32 devices in a mesh: groups: 2 (over x), outer: 4 (over y, core), inner: 4 (over z).
Axes of the slice: x: 2, y: 2, z: 4, core: 2. Of those that a mesh axis runs over, the one named last changes fastest.
Arguments:
- queries: bfloat16 [16384, 1024], P(('groups', 'outer', 'inner')), parts along dimension 0, may hold values from -32 to 32
- keys: bfloat16 [16384, 128], P(('groups', 'outer', 'inner')), parts along dimension 0, may hold values from -32 to 32
- values: bfloat16 [16384, 128], P(('groups', 'outer', 'inner')), parts along dimension 0, may hold values from -6 to 6
- doc_lengths: int32 [10], P('groups'), parts along dimension 0, may hold values from 1 to 2048, 8192 in all
Outputs:
- attended: bfloat16 [16384, 1024], P(('groups', 'outer', 'inner')), parts along dimension 0
The draws below stay inside these ranges and needn't reach their ends.
There are 2 independent parts, one for each index of `groups`. The reference program is written for one: setup_inputs(seed, part) draws one part's arguments, and reference() takes and returns one part's arrays. A program takes and returns all parts, laid end to end along the dimension named above; each array names one. Nothing has to cross between parts.
Inputs may be any that keep to these rules, and one draw needn't show every extreme that they name: `doc_lengths`: they sum to 8192; the longest is exactly 2048.
All inputs are finite; a program needn't handle non-finite values.
Results may differ from the reference program's by a relative error of at most 0.0041.
Values may be sent and summed in bfloat16 or wider, within the bound.
No kernel may reach another device: no remote copies, remote signals or barrier semaphores. Data moves between devices by JAX's collectives and lax.ppermute only.
A program may use at most 128 MiB of HBM per device.

```python
import math
import jax
import jax.numpy as jnp
import numpy as np
from jax import lax

HEADS = 8
HEAD = 128
SEQ = 8192
BLOCK = 2048
DOCS = 5


def draw_keys(key, part):
    key = jax.random.fold_in(key, 1)
    result = jax.random.normal(key, (SEQ, HEAD), jnp.float32)
    return jnp.clip(result, -32.0, 32.0).astype(jnp.bfloat16)


def draw_queries(key, part):
    key = jax.random.fold_in(key, 2)
    result = jax.random.normal(key, (SEQ, HEADS, HEAD), jnp.float32)
    return jnp.clip(result, -32.0, 32.0).reshape(SEQ, HEADS * HEAD).astype(jnp.bfloat16)


def level_of(key, extent, pieces, smallest, largest):
    factor_of = 1.0
    for position, shards_of in pieces:
        heights = jax.random.uniform(jax.random.fold_in(jax.random.fold_in(key, 6), position), (shards_of,), jnp.float32, smallest / len(pieces), largest / len(pieces))
        factor_of = factor_of * jnp.repeat(jnp.exp(heights), extent[position] // shards_of).reshape((-1,) + (1,) * (len(extent) - 1 - position))
    return factor_of


def length_profile(count, total, bound, skew):
    weights = [(1 << 20) // math.isqrt(grade ** skew) + 1 for grade in range(2, count + 1)]
    surplus, counts = total - bound - (count - 1), [1] * (count - 1)
    while surplus > 0:
        movable = [i for i in range(count - 1) if counts[i] < bound]
        whole, budget = sum([weights[i] for i in movable]), surplus
        for i in movable:
            addition = min(bound - counts[i], max(1, budget * weights[i] // whole), surplus)
            counts[i] = counts[i] + addition
            surplus = surplus - addition
    return np.array([bound] + counts)


def ragged_sizes(own_key, count, total, bound, slope):
    if count == 2:
        one = jax.random.randint(own_key, (), max(1, total - bound), min(bound, total - 1) + 1)
        return jnp.stack([one, total - one])
    tallies = jnp.asarray(length_profile(count, total, bound, slope), jnp.int32)
    twos = (count - 1) // 2
    giver, sink = tallies[1:1 + 2 * twos:2], tallies[2:2 + 2 * twos:2]
    slack = jnp.minimum(giver - 1, bound - sink)
    moved = jax.random.randint(jax.random.fold_in(own_key, 1), (twos,), 0, 1 << 20) % (slack + 1)
    tallies = tallies.at[1:1 + 2 * twos:2].set(giver - moved).at[2:2 + 2 * twos:2].set(sink + moved)
    return tallies[jax.random.permutation(jax.random.fold_in(own_key, 2), count)]


def gaussian(key, extent, width, bound, split=(), held_as=jnp.bfloat16):
    gain = level_of(key, extent, split, -0.22, 0.18) if split else 1.0
    values = jax.random.normal(key, extent, jnp.float32) * width * gain
    return jnp.minimum(jnp.maximum(values, -bound), bound).astype(held_as)


def setup_inputs(seed: int = 0, part: int = 0) -> dict:
    arg_keys = jax.random.split(jax.random.key(seed), 5)
    part_splits = jax.random.split(jax.random.fold_in(arg_keys[4], part), 5)
    return {
        "queries": draw_queries(jax.random.fold_in(jax.random.fold_in(arg_keys[4], part), 71), part),
        "keys": draw_keys(jax.random.fold_in(jax.random.fold_in(arg_keys[4], part), 71), part),
        "values": gaussian(part_splits[2], (SEQ, HEAD), 1.0, 6.0, ((0, 16),)),
        "doc_lengths": ragged_sizes(part_splits[3], DOCS, SEQ, BLOCK, 1).astype(jnp.int32),
    }


def reference(queries, keys, values, doc_lengths):
    seq_len = queries.shape[0]
    doc_ends = jnp.cumsum(doc_lengths).astype(jnp.int32)
    positions = jnp.arange(seq_len, dtype=jnp.int32)
    doc_ids = lax.optimization_barrier(jnp.sum((positions[:, None] >= doc_ends[None, :]).astype(jnp.int32), axis=1))
    query_block = min(512, seq_len)
    window_len = min(seq_len, BLOCK + query_block)
    score_scale = 1.0 / math.sqrt(HEAD)

    def one_block(block_index):
        query_start = (block_index * query_block).astype(jnp.int32)
        key_start = jnp.clip(query_start + query_block - window_len, 0, seq_len - window_len).astype(jnp.int32)
        query_part = lax.dynamic_slice_in_dim(queries, query_start, query_block, 0).reshape(query_block, HEADS, HEAD)
        key_part = lax.dynamic_slice_in_dim(keys, key_start, window_len, 0)
        value_part = lax.dynamic_slice_in_dim(values, key_start, window_len, 0)
        query_pos = query_start + jnp.arange(query_block, dtype=jnp.int32)
        key_pos = key_start + jnp.arange(window_len, dtype=jnp.int32)
        query_doc = lax.dynamic_slice_in_dim(doc_ids, query_start, query_block, 0)
        key_doc = lax.dynamic_slice_in_dim(doc_ids, key_start, window_len, 0)
        allowed = (query_doc[:, None] == key_doc[None, :]) & (key_pos[None, :] <= query_pos[:, None])
        scores = jnp.einsum('qhd,kd->qhk', query_part.astype(jnp.float32), key_part.astype(jnp.float32)) * score_scale
        scores = jnp.where(allowed[:, None, :], scores, -1e+30)
        row_max = lax.optimization_barrier(jnp.max(scores, axis=2, keepdims=True))
        weights = jnp.where(allowed[:, None, :], jnp.exp(scores - row_max), 0.0)
        row_total = lax.optimization_barrier(jnp.sum(weights, axis=2))
        rounded = lax.optimization_barrier(weights.astype(jnp.bfloat16)).astype(jnp.float32)
        mixed_sum = jnp.einsum('qhk,kd->qhd', rounded, value_part.astype(jnp.float32))
        return (mixed_sum / row_total[:, :, None]).reshape(query_block, HEADS * HEAD).astype(jnp.bfloat16)
    blocks_out = lax.map(one_block, jnp.arange(seq_len // query_block, dtype=jnp.int32))
    return blocks_out.reshape(seq_len, HEADS * HEAD)
```

```python
import functools
import math

import jax
import jax.numpy as jnp
from jax import lax
from jax.experimental import pallas as pl
from jax.experimental.pallas import tpu as pltpu
from jax.sharding import PartitionSpec as P

HEAD = 128
FAR_BELOW = -1e30
EXP2_SCALE = math.log2(math.e) / math.sqrt(HEAD)
SEQ_AXES = ("outer", "inner")


def shifted(value, steps):
    count = lax.axis_size(SEQ_AXES)
    return lax.ppermute(value, SEQ_AXES, [(source, source + steps) for source in range(count - steps)])


def doc_start(doc_ref, position):
    end = jnp.int32(0)
    start = jnp.zeros_like(position)
    for doc in range(doc_ref.shape[0]):
        end = end + doc_ref[doc]
        start = jnp.where(position >= end, end, start)
    return start


def stage(back, first, last, reach, heads, tile, *refs):
    refs = list(refs)
    pos_ref, doc_ref, q_ref, kv_ref = refs[:4]
    refs = refs[4:]
    if first:
        acc_in = stat_in = None
    else:
        acc_in, stat_in = refs[:2]
        refs = refs[2:]
    if last:
        (out_ref,) = refs
    else:
        acc_out, stat_out = refs
    rows = q_ref.shape[0]
    first_row = pos_ref[0]
    key_start = first_row - back * rows
    lanes = lax.broadcasted_iota(jnp.int32, (tile, HEAD), 1)

    def column(stats, index):
        return jnp.broadcast_to(stats[:, index : index + 1], (tile, HEAD))

    def process(row0, key0, key1, masked):
        rs = pl.ds(row0, tile)
        width = key1 - key0
        k = kv_ref[0, key0:key1, :]
        v = kv_ref[1, key0:key1, :]
        v = jnp.concatenate([v, jnp.ones_like(v)], axis=1)
        if masked:
            row_pos = first_row + row0 + lax.broadcasted_iota(jnp.int32, (tile, 1), 0)
            low = doc_start(doc_ref, row_pos)
            key_pos = key_start + key0 + lax.broadcasted_iota(jnp.int32, (tile, width), 1)
            allowed = key_pos >= low
            if back == 0:
                allowed = allowed & (key_pos <= row_pos)
        stats = None if first else stat_in[rs, :]
        new_stats = jnp.zeros((tile, HEAD), jnp.float32)

        def scores(h):
            s = lax.dot_general(
                q_ref[rs, h * HEAD : (h + 1) * HEAD],
                k,
                (((1,), (1,)), ((), ())),
                preferred_element_type=jnp.float32,
            )
            return s

        ahead = scores(0)
        for h in range(heads):
            s = ahead
            if h + 1 < heads:
                ahead = scores(h + 1)
            if masked:
                s = jnp.where(allowed, s, FAR_BELOW)
            top = jnp.max(s, axis=1, keepdims=True)
            if not first:
                old = stats[:, h : h + 1]
                top = jnp.maximum(old, top)
                factor = jnp.exp2((old - top) * EXP2_SCALE)
            p = jnp.exp2((s - top) * EXP2_SCALE).astype(jnp.bfloat16)
            pv = jnp.dot(p, v, preferred_element_type=jnp.float32)
            total = pv[:, HEAD:]
            mixed = pv[:, :HEAD]
            cs = slice(h * HEAD, (h + 1) * HEAD)
            if not first:
                mixed = mixed + acc_in[rs, cs] * factor
                total = total + column(stats, heads + h) * factor
            if last:
                out_ref[rs, cs] = (mixed / total).astype(out_ref.dtype)
            else:
                acc_out[rs, cs] = mixed
                new_stats = jnp.where(lanes == h, top, new_stats)
                new_stats = jnp.where(lanes == heads + h, total, new_stats)
        if not last:
            stat_out[rs, :] = new_stats

    def keep(row0):
        rs = pl.ds(row0, tile)
        stats = stat_in[rs, :]
        if last:
            for h in range(heads):
                cs = slice(h * HEAD, (h + 1) * HEAD)
                out_ref[rs, cs] = (acc_in[rs, cs] / column(stats, heads + h)).astype(out_ref.dtype)
        else:
            acc_out[rs, :] = acc_in[rs, :]
            stat_out[rs, :] = stats

    for row0 in range(0, rows, tile):
        if back == 0:
            process(row0, 0, row0 + tile, True)
            continue
        key0 = row0 if back == reach else 0
        low_first = doc_start(doc_ref, first_row + row0)
        low_last = doc_start(doc_ref, first_row + row0 + tile - 1)
        needed = low_first < key_start + rows
        full = low_last <= key_start + key0

        pl.when(needed & full)(functools.partial(process, row0, key0, rows, False))
        pl.when(needed & jnp.logical_not(full))(functools.partial(process, row0, key0, rows, True))
        pl.when(jnp.logical_not(needed))(functools.partial(keep, row0))


def take_in(back, first, last, reach, position, docs, queries, kv, state):
    rows, width = queries.shape
    heads = width // HEAD
    tile = min(256, rows)
    vmem = pl.BlockSpec(memory_space=pltpu.VMEM)
    smem = pl.BlockSpec(memory_space=pltpu.SMEM)
    if last:
        out_shape = jax.ShapeDtypeStruct((rows, width), jnp.bfloat16)
        out_specs = vmem
    else:
        out_shape = (
            jax.ShapeDtypeStruct((rows, width), jnp.float32),
            jax.ShapeDtypeStruct((rows, HEAD), jnp.float32),
        )
        out_specs = (vmem, vmem)
    state = () if first else state
    return pl.pallas_call(
        functools.partial(stage, back, first, last, reach, heads, tile),
        out_shape=out_shape,
        in_specs=[smem, smem, vmem, vmem] + [vmem] * len(state),
        out_specs=out_specs,
        compiler_params=pltpu.CompilerParams(vmem_limit_bytes=32 * 1024 * 1024),
        cost_estimate=pl.CostEstimate(
            flops=4 * rows * rows * width,
            bytes_accessed=8 * rows * width,
            transcendentals=rows * rows * heads,
        ),
        name=f"take_in_{back}",
    )(position, docs, queries, kv, *state)


def shards(queries, keys, values, doc_lengths):
    rows = queries.shape[0]
    reach = lax.axis_size("inner")
    position = (lax.axis_index(SEQ_AXES) * rows).astype(jnp.int32).reshape(1)
    kv = jnp.stack([keys, values])
    order = [reach, 1] + list(range(reach - 1, 1, -1))
    moved = {back: shifted(kv, back) for back in order}
    state = take_in(0, True, False, reach, position, doc_lengths, queries, kv, None)
    for back in order:
        state = take_in(back, False, back == order[-1], reach, position, doc_lengths, queries, moved[back], state)
    return state


def solution(mesh):
    return jax.shard_map(
        shards,
        mesh=mesh,
        in_specs=(
            P(("groups", "outer", "inner"), None),
            P(("groups", "outer", "inner"), None),
            P(("groups", "outer", "inner"), None),
            P("groups"),
        ),
        out_specs=P(("groups", "outer", "inner"), None),
        check_vma=False,
    )
```

```python
import functools
import math

import jax
import jax.numpy as jnp
from jax import lax
from jax.experimental import pallas as pl
from jax.experimental.pallas import tpu as pltpu
from jax.sharding import PartitionSpec as P

HEAD = 128
ONES = 16
FAR_BELOW = -1e30
EXP2_SCALE = math.log2(math.e) / math.sqrt(HEAD)
SEQ_AXES = ("outer", "inner")
def shifted(value, steps):
    count = lax.axis_size(SEQ_AXES)
    return lax.ppermute(value, SEQ_AXES, [(source, source + steps) for source in range(count - steps)])


def doc_start(doc_ref, position):
    end = jnp.int32(0); start = jnp.zeros_like(position)
    for doc in range(doc_ref.shape[0]):
        end = end + doc_ref[doc]
        start = jnp.where(position >= end, end, start)
    return start
def stage(back, first, last, reach, heads, tile, *refs):
    refs = list(refs)
    pos_ref, doc_ref, q_ref, kv_ref = refs[:4]
    refs = refs[4:]
    if first: acc_in = stat_in = None
    else:
        acc_in, stat_in = refs[:2]; refs = refs[2:]
    if last: (out_ref,) = refs
    else: acc_out, stat_out = refs
    rows = q_ref.shape[0]
    first_row = pos_ref[0]
    key_start = first_row - back * rows
    def process(row0, key0, key1, masked):
        rs = slice(row0, row0+tile)
        width = key1 - key0
        k = kv_ref[0, key0:key1, :]
        v = kv_ref[1, key0:key1, :].T
        v = jnp.concatenate([v, jnp.ones((ONES, width), v.dtype)], axis=0)
        if masked:
            row_pos = first_row + row0 + lax.broadcasted_iota(jnp.int32, (1, tile), 1)
            low = doc_start(doc_ref, row_pos)
            key_pos = key_start + key0 + lax.broadcasted_iota(jnp.int32, (width, tile), 0)
            allowed = key_pos >= low
            if back == 0: allowed = allowed & (key_pos <= row_pos)
        def scores(h):
            return lax.dot_general(k, q_ref[rs, h*HEAD:(h+1)*HEAD], (((1,), (1,)), ((), ())), preferred_element_type=jnp.float32)
        ahead = scores(0)
        for h in range(heads):
            s = ahead
            if h + 1 < heads: ahead = scores(h+1)
            if masked: s = jnp.where(allowed, s, FAR_BELOW)
            top = jnp.max(s, axis=0, keepdims=True)
            if not first:
                old = stat_in[h:h+1, rs]
                top = jnp.maximum(old, top)
                factor = jnp.exp2((old - top) * EXP2_SCALE)
            p = jnp.exp2((s - top) * EXP2_SCALE).astype(jnp.bfloat16)
            pv = lax.dot_general(v, p, (((1,), (0,)), ((), ())), preferred_element_type=jnp.float32)
            total = pv[HEAD:HEAD+1]
            mixed = pv[:HEAD]
            hs = slice(h*HEAD, (h+1)*HEAD)
            if not first:
                mixed = mixed + acc_in[hs, rs] * factor
                total = total + stat_in[heads+h:heads+h+1, rs] * factor
            if last:
                out_ref[rs, hs] = (mixed / total).T.astype(out_ref.dtype)
            else:
                acc_out[hs, rs] = mixed
                stat_out[h:h+1, rs] = top
                stat_out[heads+h:heads+h+1, rs] = total
    def keep(row0):
        rs = slice(row0, row0+tile)
        if last:
            for h in range(heads):
                hs = slice(h*HEAD, (h+1)*HEAD)
                out_ref[rs, hs] = (acc_in[hs, rs] / stat_in[heads+h:heads+h+1, rs]).T.astype(out_ref.dtype)
        else:
            acc_out[:, rs] = acc_in[:, rs]
            stat_out[:, rs] = stat_in[:, rs]
    for row0 in range(0, rows, tile):
        if back == 0:
            process(row0, 0, row0 + tile, True); continue
        key0 = row0 if back == reach else 0
        low_first = doc_start(doc_ref, first_row + row0)
        low_last = doc_start(doc_ref, first_row + row0 + tile - 1)
        needed = low_first < key_start + rows
        full = low_last <= key_start + key0
        pl.when(needed & full)(functools.partial(process, row0, key0, rows, False))
        pl.when(needed & jnp.logical_not(full))(functools.partial(process, row0, key0, rows, True))
        pl.when(jnp.logical_not(needed))(functools.partial(keep, row0))
def take_in(back, first, last, reach, position, docs, queries, kv, state, tile=512):
    rows, width = queries.shape
    heads = width // HEAD
    vmem = pl.BlockSpec(memory_space=pltpu.VMEM); smem = pl.BlockSpec(memory_space=pltpu.SMEM)
    if last:
        out_shape = jax.ShapeDtypeStruct((rows, width), jnp.bfloat16); out_specs = vmem
    else:
        out_shape = (jax.ShapeDtypeStruct((width, rows), jnp.float32), jax.ShapeDtypeStruct((2*heads, rows), jnp.float32)); out_specs = (vmem, vmem)
    state = () if first else state
    return pl.pallas_call(functools.partial(stage, back, first, last, reach, heads, min(tile,rows)), out_shape=out_shape,
        in_specs=[smem, smem, vmem, vmem] + [vmem]*len(state), out_specs=out_specs,
        compiler_params=pltpu.CompilerParams(vmem_limit_bytes=32*1024*1024),
        cost_estimate=pl.CostEstimate(flops=4*rows*rows*width, bytes_accessed=8*rows*width, transcendentals=rows*rows*heads),
        name=f"take_in_{back}")(position, docs, queries, kv, *state)


def shards(queries, keys, values, doc_lengths):
    rows = queries.shape[0]
    reach = lax.axis_size("inner")
    position = (lax.axis_index(SEQ_AXES) * rows).astype(jnp.int32).reshape(1)
    kv = jnp.stack([keys, values])
    order = [reach, 1] + list(range(reach - 1, 1, -1))
    moved = {back: shifted(kv, back) for back in order}
    state = take_in(0, True, False, reach, position, doc_lengths, queries, kv, None)
    for back in order:
        state = take_in(back, False, back == order[-1], reach, position, doc_lengths, queries, moved[back], state)
    return state


def solution(mesh):
    return jax.shard_map(
        shards,
        mesh=mesh,
        in_specs=(
            P(("groups", "outer", "inner"), None),
            P(("groups", "outer", "inner"), None),
            P(("groups", "outer", "inner"), None),
            P("groups"),
        ),
        out_specs=P(("groups", "outer", "inner"), None),
        check_vma=False,
    )
```

```python
import functools
import math

import jax
import jax.numpy as jnp
from jax import lax
from jax.experimental import pallas as pl
from jax.experimental.pallas import tpu as pltpu
from jax.sharding import PartitionSpec as P

HEAD = 128
ONES = 16
FAR_BELOW = -1e30
LIMIT = 2.0**60
EXP2_SCALE = math.log2(math.e) / math.sqrt(HEAD)
SEQ_AXES = ("outer", "inner")
VMEM = pl.BlockSpec(memory_space=pltpu.VMEM)
NT = (((1,), (1,)), ((), ()))
NN = (((1,), (0,)), ((), ()))


def shifted(value, steps):
    count = lax.axis_size(SEQ_AXES)
    return lax.ppermute(value, SEQ_AXES, [(source, source + steps) for source in range(count - steps)])


def document_starts(docs_ref, low_out):
    first_row = lax.axis_index(SEQ_AXES) * low_out.shape[1]
    position = first_row + lax.broadcasted_iota(jnp.int32, low_out.shape, 1)
    end = jnp.int32(0)
    start = jnp.zeros_like(position)
    for doc in range(docs_ref.shape[0]):
        end = end + docs_ref[doc]
        start = jnp.where(position >= end, end, start)
    low_out[...] = (start - first_row).astype(jnp.float32)


def query_lows(docs, rows):
    return pl.pallas_call(
        document_starts,
        out_shape=jax.ShapeDtypeStruct((8, rows), jnp.float32),
        in_specs=[pl.BlockSpec(memory_space=pltpu.SMEM)],
        out_specs=VMEM,
        compiler_params=pltpu.CompilerParams(vmem_limit_bytes=8 * 1024 * 1024),
        name="document_starts",
    )(docs)


def stage(back, first, last, reach, heads, tile, *refs):
    low_ref, q_ref, kv_ref, *refs = refs
    if not first:
        acc_in, stat_in, *refs = refs
    if last:
        out_ref, vt_ref = refs
    else:
        acc_out, stat_out, vt_ref = refs
    rows = q_ref.shape[0]

    def allowed_pairs(q0, q1, k0, k1):
        low = low_ref[0:1, q0:q1].astype(jnp.int32) + (back * rows - k0)
        key = lax.broadcasted_iota(jnp.int32, (k1 - k0, q1 - q0), 0)
        allowed = key >= low
        if back == 0:
            query = q0 - k0 + lax.broadcasted_iota(jnp.int32, (1, q1 - q0), 1)
            allowed = allowed & (key <= query)
        return allowed

    def finish(h, q0, q1, mixed, total, top):
        if isinstance(h, int):
            hs = slice(h * HEAD, (h + 1) * HEAD)
        else:
            hs = pl.ds(pl.multiple_of(h * HEAD, HEAD), HEAD)
        if last:
            out_ref[q0:q1, hs] = (mixed * (1.0 / total)).astype(out_ref.dtype).T
        else:
            acc_out[hs, q0:q1] = mixed
            stat_out[h, 0:1, q0:q1] = top
            stat_out[h, 1:2, q0:q1] = total

    def flow(masked):
        items = []
        for h in range(heads):
            for q0 in range(0, rows, tile):
                k0 = q0 if back == reach else 0
                k1 = q0 + tile if back == 0 else rows
                items.append((h, q0, k0, k1))
        masks, scores, weights, tops = {}, {}, {}, {}
        worst = jnp.zeros((1, tile), jnp.float32)
        for step in range(len(items) + 2):
            if step < len(items):
                h, q0, k0, k1 = items[step]
                s = lax.dot_general(
                    kv_ref[0, k0:k1, :],
                    q_ref[q0 : q0 + tile, h * HEAD : (h + 1) * HEAD],
                    NT,
                    preferred_element_type=jnp.float32,
                )
                if masked:
                    if q0 not in masks:
                        masks[q0] = allowed_pairs(q0, q0 + tile, k0, k1)
                    s = jnp.where(masks[q0], s, FAR_BELOW)
                scores[step] = s
            if 1 <= step <= len(items):
                h, q0, k0, k1 = items[step - 1]
                s = scores.pop(step - 1)
                top = jnp.max(s, axis=0, keepdims=True) if first else stat_in[h, 0:1, q0 : q0 + tile]
                tops[step - 1] = top
                weights[step - 1] = jnp.exp2((s - top) * EXP2_SCALE).astype(jnp.bfloat16)
            if 2 <= step:
                h, q0, k0, k1 = items[step - 2]
                q1 = q0 + tile
                sums = lax.dot_general(
                    vt_ref[:, k0:k1], weights.pop(step - 2), NN, preferred_element_type=jnp.float32
                )
                mixed = sums[:HEAD]
                total = sums[HEAD : HEAD + 1]
                if not first:
                    worst = jnp.maximum(worst, total)
                    mixed = mixed + acc_in[h * HEAD : (h + 1) * HEAD, q0:q1]
                    total = total + stat_in[h, 1:2, q0:q1]
                finish(h, q0, q1, mixed, total, tops.pop(step - 2))
        if not first:
            pl.when(jnp.logical_not(jnp.max(worst) < LIMIT))(rescaled)

    def rescaled():
        allowed = allowed_pairs(0, rows, 0, rows)

        def one_head(h, carry):
            hs = pl.ds(pl.multiple_of(h * HEAD, HEAD), HEAD)
            s = lax.dot_general(kv_ref[0], q_ref[:, hs], NT, preferred_element_type=jnp.float32)
            s = jnp.where(allowed, s, FAR_BELOW)
            old = stat_in[h, 0:1, :]
            top = jnp.maximum(old, jnp.max(s, axis=0, keepdims=True))
            factor = jnp.exp2((old - top) * EXP2_SCALE)
            p = jnp.exp2((s - top) * EXP2_SCALE).astype(jnp.bfloat16)
            sums = lax.dot_general(vt_ref[...], p, NN, preferred_element_type=jnp.float32)
            mixed = sums[:HEAD] + acc_in[hs, :] * factor
            total = sums[HEAD : HEAD + 1] + stat_in[h, 1:2, :] * factor
            finish(h, 0, rows, mixed, total, top)
            return carry

        lax.fori_loop(0, heads, one_head, 0)

    def keep():
        def one_head(h, carry):
            hs = pl.ds(pl.multiple_of(h * HEAD, HEAD), HEAD)
            finish(h, 0, rows, acc_in[hs, :], stat_in[h, 1:2, :], stat_in[h, 0:1, :])
            return carry

        lax.fori_loop(0, heads, one_head, 0)

    def work(masked):
        vt_ref[:HEAD, :] = kv_ref[1].T
        vt_ref[HEAD:, :] = jnp.ones((ONES, rows), vt_ref.dtype)
        flow(masked)

    if first:
        work(True)
        return
    low = low_ref[...]
    needed = jnp.min(low) < (1 - back) * rows
    if back == reach:
        full = jnp.bool_(False)
    else:
        full = jnp.max(low) <= -back * rows
        pl.when(needed & full)(functools.partial(work, False))
    pl.when(needed & jnp.logical_not(full))(functools.partial(work, True))
    pl.when(jnp.logical_not(needed))(keep)


def take_in(back, first, last, reach, low, queries, kv, state):
    rows, width = queries.shape
    heads = width // HEAD
    state = () if first else state
    if last:
        out_shape = jax.ShapeDtypeStruct((rows, width), jnp.bfloat16)
        out_specs = VMEM
    else:
        out_shape = (
            jax.ShapeDtypeStruct((width, rows), jnp.float32),
            jax.ShapeDtypeStruct((heads, 8, rows), jnp.float32),
        )
        out_specs = (VMEM, VMEM)
    return pl.pallas_call(
        functools.partial(stage, back, first, last, reach, heads, rows),
        out_shape=out_shape,
        in_specs=[VMEM] * (3 + len(state)),
        out_specs=out_specs,
        scratch_shapes=[pltpu.VMEM((HEAD + ONES, rows), jnp.bfloat16)],
        compiler_params=pltpu.CompilerParams(vmem_limit_bytes=32 * 1024 * 1024),
        cost_estimate=pl.CostEstimate(
            flops=4 * rows * rows * width,
            bytes_accessed=8 * rows * width,
            transcendentals=rows * rows * heads,
        ),
        name=f"take_in_{back}",
    )(low, queries, kv, *state)


def shards(queries, keys, values, doc_lengths):
    reach = lax.axis_size("inner")
    rows = queries.shape[0]
    kv = jnp.stack([keys, values])
    middle = range(reach - 2, 2, -1)
    plan = [("send", reach), ("send", 1), ("send", reach - 1), *[("send", back) for back in middle], ("send", 2), ("take", 0), ("take", reach), ("take", 1), ("take", reach - 1), *[("take", back) for back in middle], ("take", 2)]
    moved = {0: kv}
    state = None
    low = query_lows(doc_lengths, rows)
    last = plan[-1][1]
    for verb, back in plan:
        if verb == "send":
            if state is not None:
                kv, state = lax.optimization_barrier((kv, state))
            moved[back] = shifted(kv, back)
        else:
            state = take_in(back, back == 0, back == last, reach, low, queries, moved[back], state)
    return state


def solution(mesh):
    return jax.shard_map(
        shards,
        mesh=mesh,
        in_specs=(
            P(("groups", "outer", "inner"), None),
            P(("groups", "outer", "inner"), None),
            P(("groups", "outer", "inner"), None),
            P("groups"),
        ),
        out_specs=P(("groups", "outer", "inner"), None),
        check_vma=False,
    )
```

```python
import functools
import math

import jax
import jax.numpy as jnp
from jax import lax
from jax.experimental import pallas as pl
from jax.experimental.pallas import tpu as pltpu
from jax.sharding import PartitionSpec as P

HEAD = 128
ONES = 16
FAR_BELOW = -1e30
LIMIT = 2.0**60
EXP2_SCALE = math.log2(math.e) / math.sqrt(HEAD)
SEQ_AXES = ("outer", "inner")
VMEM = pl.BlockSpec(memory_space=pltpu.VMEM)
NT = (((1,), (1,)), ((), ()))
NN = (((1,), (0,)), ((), ()))


def sent(value, pairs):
    return lax.ppermute(value, SEQ_AXES, pairs)


def document_starts(docs_ref, low_out):
    first_row = lax.axis_index(SEQ_AXES) * low_out.shape[1]
    position = first_row + lax.broadcasted_iota(jnp.int32, low_out.shape, 1)
    end = jnp.int32(0)
    start = jnp.zeros_like(position)
    for doc in range(docs_ref.shape[0]):
        end = end + docs_ref[doc]
        start = jnp.where(position >= end, end, start)
    low_out[...] = (start - first_row).astype(jnp.float32)


def query_lows(docs, rows):
    return pl.pallas_call(
        document_starts,
        out_shape=jax.ShapeDtypeStruct((8, rows), jnp.float32),
        in_specs=[pl.BlockSpec(memory_space=pltpu.SMEM)],
        out_specs=VMEM,
        compiler_params=pltpu.CompilerParams(vmem_limit_bytes=8 * 1024 * 1024),
        name="document_starts",
    )(docs)


def stage(backs, first, last, window, heads, tile, *refs):
    low_ref, q_ref, kv_ref, *refs = refs
    if not first:
        acc_in, stat_in, *refs = refs
    if last:
        out_ref, vt_ref = refs
    else:
        acc_out, stat_out, vt_ref = refs
    rows = q_ref.shape[0]
    if backs[0] == backs[1]:
        back = backs[0]
    else:
        back = backs[0] + (backs[1] - backs[0]) * lax.rem(lax.axis_index("inner"), 2)

    def allowed_pairs(q0, q1, k0, k1):
        low = low_ref[0:1, q0:q1].astype(jnp.int32) + (back * rows - k0)
        key = lax.broadcasted_iota(jnp.int32, (k1 - k0, q1 - q0), 0)
        allowed = key >= low
        if first:
            query = q0 - k0 + lax.broadcasted_iota(jnp.int32, (1, q1 - q0), 1)
            allowed = allowed & (key <= query)
        return allowed

    def finish(h, q0, q1, mixed, total, top):
        if isinstance(h, int):
            hs = slice(h * HEAD, (h + 1) * HEAD)
        else:
            hs = pl.ds(pl.multiple_of(h * HEAD, HEAD), HEAD)
        if last:
            out_ref[q0:q1, hs] = (mixed * (1.0 / total)).astype(out_ref.dtype).T
        else:
            acc_out[hs, q0:q1] = mixed
            stat_out[h, 0:1, q0:q1] = top
            stat_out[h, 1:2, q0:q1] = total

    def flow(masked):
        items = []
        for h in range(heads):
            for q0 in range(0, rows, tile):
                k0 = q0 if window else 0
                k1 = q0 + tile if first else rows
                items.append((h, q0, k0, k1))
        masks, scores, weights, tops = {}, {}, {}, {}
        worst = jnp.zeros((1, tile), jnp.float32)
        for step in range(len(items) + 2):
            if step < len(items):
                h, q0, k0, k1 = items[step]
                s = lax.dot_general(
                    kv_ref[0, k0:k1, :],
                    q_ref[q0 : q0 + tile, h * HEAD : (h + 1) * HEAD],
                    NT,
                    preferred_element_type=jnp.float32,
                )
                if masked:
                    if q0 not in masks:
                        masks[q0] = allowed_pairs(q0, q0 + tile, k0, k1)
                    s = jnp.where(masks[q0], s, FAR_BELOW)
                scores[step] = s
            if 1 <= step <= len(items):
                h, q0, k0, k1 = items[step - 1]
                s = scores.pop(step - 1)
                top = jnp.max(s, axis=0, keepdims=True) if first else stat_in[h, 0:1, q0 : q0 + tile]
                tops[step - 1] = top
                weights[step - 1] = jnp.exp2((s - top) * EXP2_SCALE).astype(jnp.bfloat16)
            if 2 <= step:
                h, q0, k0, k1 = items[step - 2]
                q1 = q0 + tile
                sums = lax.dot_general(
                    vt_ref[:, k0:k1], weights.pop(step - 2), NN, preferred_element_type=jnp.float32
                )
                mixed = sums[:HEAD]
                total = sums[HEAD : HEAD + 1]
                if not first:
                    worst = jnp.maximum(worst, total)
                    mixed = mixed + acc_in[h * HEAD : (h + 1) * HEAD, q0:q1]
                    total = total + stat_in[h, 1:2, q0:q1]
                finish(h, q0, q1, mixed, total, tops.pop(step - 2))
        if not first:
            pl.when(jnp.logical_not(jnp.max(worst) < LIMIT))(rescaled)

    def rescaled():
        allowed = allowed_pairs(0, rows, 0, rows)

        def one_head(h, carry):
            hs = pl.ds(pl.multiple_of(h * HEAD, HEAD), HEAD)
            s = lax.dot_general(kv_ref[0], q_ref[:, hs], NT, preferred_element_type=jnp.float32)
            s = jnp.where(allowed, s, FAR_BELOW)
            old = stat_in[h, 0:1, :]
            top = jnp.maximum(old, jnp.max(s, axis=0, keepdims=True))
            factor = jnp.exp2((old - top) * EXP2_SCALE)
            p = jnp.exp2((s - top) * EXP2_SCALE).astype(jnp.bfloat16)
            sums = lax.dot_general(vt_ref[...], p, NN, preferred_element_type=jnp.float32)
            mixed = sums[:HEAD] + acc_in[hs, :] * factor
            total = sums[HEAD : HEAD + 1] + stat_in[h, 1:2, :] * factor
            finish(h, 0, rows, mixed, total, top)
            return carry

        lax.fori_loop(0, heads, one_head, 0)

    def keep():
        def one_head(h, carry):
            hs = pl.ds(pl.multiple_of(h * HEAD, HEAD), HEAD)
            finish(h, 0, rows, acc_in[hs, :], stat_in[h, 1:2, :], stat_in[h, 0:1, :])
            return carry

        lax.fori_loop(0, heads, one_head, 0)

    def work(masked):
        vt_ref[:HEAD, :] = kv_ref[1].T
        vt_ref[HEAD:, :] = jnp.ones((ONES, rows), vt_ref.dtype)
        flow(masked)

    if first:
        work(True)
        return
    low = low_ref[...]
    first_key = (-back * rows) if isinstance(back, int) else (-back * rows).astype(jnp.float32)
    needed = jnp.min(low) < first_key + rows
    if window:
        full = jnp.bool_(False)
    else:
        full = jnp.max(low) <= first_key
        pl.when(needed & full)(functools.partial(work, False))
    pl.when(needed & jnp.logical_not(full))(functools.partial(work, True))
    pl.when(jnp.logical_not(needed))(keep)


def take_in(backs, first, last, window, low, queries, kv, state, name):
    rows, width = queries.shape
    heads = width // HEAD
    state = () if first else state
    if last:
        out_shape = jax.ShapeDtypeStruct((rows, width), jnp.bfloat16)
        out_specs = VMEM
    else:
        out_shape = (
            jax.ShapeDtypeStruct((width, rows), jnp.float32),
            jax.ShapeDtypeStruct((heads, 8, rows), jnp.float32),
        )
        out_specs = (VMEM, VMEM)
    return pl.pallas_call(
        functools.partial(stage, backs, first, last, window, heads, rows),
        out_shape=out_shape,
        in_specs=[VMEM] * (3 + len(state)),
        out_specs=out_specs,
        scratch_shapes=[pltpu.VMEM((HEAD + ONES, rows), jnp.bfloat16)],
        compiler_params=pltpu.CompilerParams(vmem_limit_bytes=32 * 1024 * 1024),
        cost_estimate=pl.CostEstimate(
            flops=4 * rows * rows * width,
            bytes_accessed=8 * rows * width,
            transcendentals=rows * rows * heads,
        ),
        name=name,
    )(low, queries, kv, *state)


def shards(queries, keys, values, doc_lengths):
    reach = lax.axis_size("inner")
    count = lax.axis_size(SEQ_AXES)
    rows = queries.shape[0]
    evens = range(2, reach - 1, 2)
    kv = jnp.stack([keys, values])
    low = query_lows(doc_lengths, rows)
    shift = {k: sent(kv, [(d, d + k) for d in range(count - k)]) for k in evens}
    beside = sent(kv, [(d, d + (reach - 1 if d % 2 else 1)) for d in range(count) if d % 2 == 0 or d + reach - 1 < count])
    window = sent(kv, [(d, d + reach) for d in range(count - reach)])
    state = take_in((0, 0), True, False, False, low, queries, kv, None, "take_own")
    state = take_in((reach, reach), False, False, True, low, queries, window, state, "take_window")
    swap = {}
    for k in evens:
        source = shift[k]
        swap[k] = sent(source, [(d, d + 1 - 2 * (d % 2)) for d in range(k, count)])
    state = take_in((reach - 1, 1), False, False, False, low, queries, beside, state, "take_beside")
    for k in evens:
        state = take_in((k, k), False, False, False, low, queries, shift[k], state, "take_shift")
        state = take_in((k - 1, k + 1), False, k == evens[-1], False, low, queries, swap[k], state, "take_swap")
    return state


def solution(mesh):
    return jax.shard_map(
        shards,
        mesh=mesh,
        in_specs=(
            P(("groups", "outer", "inner"), None),
            P(("groups", "outer", "inner"), None),
            P(("groups", "outer", "inner"), None),
            P("groups"),
        ),
        out_specs=P(("groups", "outer", "inner"), None),
        check_vma=False,
    )
```

```python
import functools
import math

import jax
import jax.numpy as jnp
from jax import lax
from jax.experimental import pallas as pl
from jax.experimental.pallas import tpu as pltpu
from jax.sharding import PartitionSpec as P

HEAD = 128
ONES = 16
FAR_BELOW = -1e30
LIMIT = 2.0**60
EXP2_SCALE = math.log2(math.e) / math.sqrt(HEAD)
SEQ_AXES = ("outer", "inner")
VMEM = pl.BlockSpec(memory_space=pltpu.VMEM)
NT = (((1,), (1,)), ((), ()))
NN = (((1,), (0,)), ((), ()))


def sent(value, pairs):
    return lax.ppermute(value, SEQ_AXES, pairs)


def document_starts(docs_ref, low_out):
    first_row = lax.axis_index(SEQ_AXES) * low_out.shape[1]
    position = first_row + lax.broadcasted_iota(jnp.int32, low_out.shape, 1)
    end = jnp.int32(0)
    start = jnp.zeros_like(position)
    for doc in range(docs_ref.shape[0]):
        end = end + docs_ref[doc]
        start = jnp.where(position >= end, end, start)
    low_out[...] = (start - first_row).astype(jnp.float32)


def query_lows(docs, rows):
    return pl.pallas_call(
        document_starts,
        out_shape=jax.ShapeDtypeStruct((8, rows), jnp.float32),
        in_specs=[pl.BlockSpec(memory_space=pltpu.SMEM)],
        out_specs=VMEM,
        compiler_params=pltpu.CompilerParams(vmem_limit_bytes=8 * 1024 * 1024),
        name="document_starts",
    )(docs)


def stage(backs, first, last, window, heads, tile, *refs):
    low_ref, q_ref, kv_ref, *refs = refs
    if not first:
        acc_in, stat_in, *refs = refs
    if last:
        out_ref, vt_ref, bias_ref = refs
    else:
        acc_out, stat_out, vt_ref, bias_ref = refs
    rows = q_ref.shape[0]
    if backs[0] == backs[1]:
        back = backs[0]
    else:
        back = backs[0] + (backs[1] - backs[0]) * lax.rem(lax.axis_index("inner"), 2)

    def allowed_pairs(q0, q1, k0, k1):
        low = low_ref[0:1, q0:q1].astype(jnp.int32) + (back * rows - k0)
        key = lax.broadcasted_iota(jnp.int32, (k1 - k0, q1 - q0), 0)
        allowed = key >= low
        if first:
            query = q0 - k0 + lax.broadcasted_iota(jnp.int32, (1, q1 - q0), 1)
            allowed = allowed & (key <= query)
        return allowed

    def finish(h, q0, q1, mixed, total, top):
        if isinstance(h, int):
            hs = slice(h * HEAD, (h + 1) * HEAD)
        else:
            hs = pl.ds(pl.multiple_of(h * HEAD, HEAD), HEAD)
        if last:
            out_ref[q0:q1, hs] = (mixed * (1.0 / total)).astype(out_ref.dtype).T
        else:
            acc_out[hs, q0:q1] = mixed
            stat_out[h, 0:1, q0:q1] = top
            stat_out[h, 1:2, q0:q1] = total

    def flow(masked):
        items = []
        for h in range(heads):
            for q0 in range(0, rows, tile):
                k0 = q0 if window else 0
                k1 = q0 + tile if first else rows
                items.append((h, q0, k0, k1))
        masks, scores, weights, tops = {}, {}, {}, {}
        worst = jnp.zeros((1, tile), jnp.float32)
        for step in range(len(items) + 2):
            if step < len(items):
                h, q0, k0, k1 = items[step]
                s = lax.dot_general(
                    kv_ref[0, k0:k1, :],
                    q_ref[q0 : q0 + tile, h * HEAD : (h + 1) * HEAD],
                    NT,
                    preferred_element_type=jnp.float32,
                )
                if first:
                    if q0 not in masks:
                        masks[q0] = allowed_pairs(q0, q0 + tile, k0, k1)
                    s = jnp.where(masks[q0], s, FAR_BELOW)
                elif masked:
                    if h == 0:
                        allowed = allowed_pairs(q0, q0 + tile, k0, k1)
                        bias_ref[k0:k1, q0 : q0 + tile] = jnp.where(allowed, 0.0, FAR_BELOW)
                    s = s + bias_ref[k0:k1, q0 : q0 + tile]
                scores[step] = s
            if 1 <= step <= len(items):
                h, q0, k0, k1 = items[step - 1]
                s = scores.pop(step - 1)
                top = jnp.max(s, axis=0, keepdims=True) if first else stat_in[h, 0:1, q0 : q0 + tile]
                tops[step - 1] = top
                weights[step - 1] = jnp.exp2((s - top) * EXP2_SCALE).astype(jnp.bfloat16)
            if 2 <= step:
                h, q0, k0, k1 = items[step - 2]
                q1 = q0 + tile
                sums = lax.dot_general(
                    vt_ref[:, k0:k1], weights.pop(step - 2), NN, preferred_element_type=jnp.float32
                )
                mixed = sums[:HEAD]
                total = sums[HEAD : HEAD + 1]
                if not first:
                    worst = jnp.maximum(worst, total)
                    mixed = mixed + acc_in[h * HEAD : (h + 1) * HEAD, q0:q1]
                    total = total + stat_in[h, 1:2, q0:q1]
                finish(h, q0, q1, mixed, total, tops.pop(step - 2))
        if not first:
            pl.when(jnp.logical_not(jnp.max(worst) < LIMIT))(rescaled)

    def rescaled():
        allowed = allowed_pairs(0, rows, 0, rows)

        def one_head(h, carry):
            hs = pl.ds(pl.multiple_of(h * HEAD, HEAD), HEAD)
            s = lax.dot_general(kv_ref[0], q_ref[:, hs], NT, preferred_element_type=jnp.float32)
            s = jnp.where(allowed, s, FAR_BELOW)
            old = stat_in[h, 0:1, :]
            top = jnp.maximum(old, jnp.max(s, axis=0, keepdims=True))
            factor = jnp.exp2((old - top) * EXP2_SCALE)
            p = jnp.exp2((s - top) * EXP2_SCALE).astype(jnp.bfloat16)
            sums = lax.dot_general(vt_ref[...], p, NN, preferred_element_type=jnp.float32)
            mixed = sums[:HEAD] + acc_in[hs, :] * factor
            total = sums[HEAD : HEAD + 1] + stat_in[h, 1:2, :] * factor
            finish(h, 0, rows, mixed, total, top)
            return carry

        lax.fori_loop(0, heads, one_head, 0)

    def keep():
        def one_head(h, carry):
            hs = pl.ds(pl.multiple_of(h * HEAD, HEAD), HEAD)
            finish(h, 0, rows, acc_in[hs, :], stat_in[h, 1:2, :], stat_in[h, 0:1, :])
            return carry

        lax.fori_loop(0, heads, one_head, 0)

    def work(masked):
        vt_ref[:HEAD, :] = kv_ref[1].T
        vt_ref[HEAD:, :] = jnp.ones((ONES, rows), vt_ref.dtype)
        flow(masked)

    if first:
        work(True)
        return
    low = low_ref[...]
    first_key = (-back * rows) if isinstance(back, int) else (-back * rows).astype(jnp.float32)
    needed = jnp.min(low) < first_key + rows
    if window:
        full = jnp.bool_(False)
    else:
        full = jnp.max(low) <= first_key
        pl.when(needed & full)(functools.partial(work, False))
    pl.when(needed & jnp.logical_not(full))(functools.partial(work, True))
    pl.when(jnp.logical_not(needed))(keep)


def take_in(backs, first, last, window, low, queries, kv, state, name):
    rows, width = queries.shape
    heads = width // HEAD
    state = () if first else state
    if last:
        out_shape = jax.ShapeDtypeStruct((rows, width), jnp.bfloat16)
        out_specs = VMEM
    else:
        out_shape = (
            jax.ShapeDtypeStruct((width, rows), jnp.float32),
            jax.ShapeDtypeStruct((heads, 8, rows), jnp.float32),
        )
        out_specs = (VMEM, VMEM)
    return pl.pallas_call(
        functools.partial(stage, backs, first, last, window, heads, rows),
        out_shape=out_shape,
        in_specs=[VMEM] * (3 + len(state)),
        out_specs=out_specs,
        scratch_shapes=[pltpu.VMEM((HEAD + ONES, rows), jnp.bfloat16), pltpu.VMEM((rows, rows), jnp.float32)],
        compiler_params=pltpu.CompilerParams(vmem_limit_bytes=32 * 1024 * 1024),
        cost_estimate=pl.CostEstimate(
            flops=4 * rows * rows * width,
            bytes_accessed=8 * rows * width,
            transcendentals=rows * rows * heads,
        ),
        name=name,
    )(low, queries, kv, *state)


def shards(queries, keys, values, doc_lengths):
    reach = lax.axis_size("inner")
    count = lax.axis_size(SEQ_AXES)
    rows = queries.shape[0]
    evens = range(2, reach - 1, 2)
    kv = jnp.stack([keys, values])
    low = query_lows(doc_lengths, rows)
    shift = {k: sent(kv, [(d, d + k) for d in range(count - k)]) for k in evens}
    kv, low = lax.optimization_barrier((kv, low))
    beside = sent(kv, [(d, d + (reach - 1 if d % 2 else 1)) for d in range(count) if d % 2 == 0 or d + reach - 1 < count])
    window = sent(kv, [(d, d + reach) for d in range(count - reach)])
    state = take_in((0, 0), True, False, False, low, queries, kv, None, "take_own")
    state = take_in((reach, reach), False, False, True, low, queries, window, state, "take_window")
    swap = {k: sent(shift[k], [(d, d + 1 - 2 * (d % 2)) for d in range(k, count)]) for k in evens}
    state = take_in((reach - 1, 1), False, False, False, low, queries, beside, state, "take_beside")
    for k in evens:
        state = take_in((k, k), False, False, False, low, queries, shift[k], state, "take_shift")
        state = take_in((k - 1, k + 1), False, k == evens[-1], False, low, queries, swap[k], state, "take_swap")
    return state


def solution(mesh):
    return jax.shard_map(
        shards,
        mesh=mesh,
        in_specs=(
            P(("groups", "outer", "inner"), None),
            P(("groups", "outer", "inner"), None),
            P(("groups", "outer", "inner"), None),
            P("groups"),
        ),
        out_specs=P(("groups", "outer", "inner"), None),
        check_vma=False,
    )
```

```python
import functools
import math

import jax
import jax.numpy as jnp
from jax import lax
from jax.experimental import pallas as pl
from jax.experimental.pallas import tpu as pltpu
from jax.sharding import PartitionSpec as P

HEAD = 128
ONES = 16
FAR_BELOW = -1e30
LIMIT = 2.0**60
EXP2_SCALE = math.log2(math.e) / math.sqrt(HEAD)
SEQ_AXES = ("outer", "inner")
VMEM = pl.BlockSpec(memory_space=pltpu.VMEM)
NT = (((1,), (1,)), ((), ()))
NN = (((1,), (0,)), ((), ()))


def sent(value, pairs):
    return lax.ppermute(value, SEQ_AXES, pairs)


def document_starts(docs_ref, low_out):
    first_row = lax.axis_index(SEQ_AXES) * low_out.shape[1]
    position = first_row + lax.broadcasted_iota(jnp.int32, low_out.shape, 1)
    end = jnp.int32(0)
    start = jnp.zeros_like(position)
    for doc in range(docs_ref.shape[0]):
        end = end + docs_ref[doc]
        start = jnp.where(position >= end, end, start)
    low_out[...] = (start - first_row).astype(jnp.float32)


def query_lows(docs, rows):
    return pl.pallas_call(
        document_starts,
        out_shape=jax.ShapeDtypeStruct((8, rows), jnp.float32),
        in_specs=[pl.BlockSpec(memory_space=pltpu.SMEM)],
        out_specs=VMEM,
        compiler_params=pltpu.CompilerParams(vmem_limit_bytes=8 * 1024 * 1024),
        name="document_starts",
    )(docs)


def stage(backs, first, last, window, heads, tile, *refs):
    low_ref, q_ref, kv_ref, *refs = refs
    if not first:
        acc_in, stat_in, *refs = refs
    if last:
        out_ref, vt_ref, bias_ref = refs
    else:
        acc_out, stat_out, vt_ref, bias_ref = refs
    rows = q_ref.shape[0]
    if backs[0] == backs[1]:
        back = backs[0]
    else:
        back = backs[0] + (backs[1] - backs[0]) * lax.rem(lax.axis_index("inner"), 2)
    first_key = (-back * rows) if isinstance(back, int) else (-back * rows).astype(jnp.float32)

    def allowed_pairs(q0, q1, k0, k1):
        low = low_ref[0:1, q0:q1].astype(jnp.int32) + (back * rows - k0)
        key = lax.broadcasted_iota(jnp.int32, (k1 - k0, q1 - q0), 0)
        allowed = key >= low
        if first:
            query = q0 - k0 + lax.broadcasted_iota(jnp.int32, (1, q1 - q0), 1)
            allowed = allowed & (key <= query)
        return allowed

    def finish(h, q0, q1, mixed, total, top):
        if isinstance(h, int):
            hs = slice(h * HEAD, (h + 1) * HEAD)
        else:
            hs = pl.ds(pl.multiple_of(h * HEAD, HEAD), HEAD)
        if last:
            out_ref[q0:q1, hs] = (mixed * (1.0 / total)).astype(out_ref.dtype).T
        else:
            acc_out[hs, q0:q1] = mixed
            stat_out[h, 0:1, q0:q1] = top
            stat_out[h, 1:2, q0:q1] = total

    def flow(masked):
        items = []
        for h in range(heads):
            for q0 in range(0, rows, tile):
                k0 = q0 if window else 0
                k1 = q0 + tile if first else rows
                items.append((h, q0, k0, k1))
        masks, scores, weights, tops = {}, {}, {}, {}
        worst = jnp.zeros((1, tile), jnp.float32)
        for step in range(len(items) + 2):
            if step < len(items):
                h, q0, k0, k1 = items[step]
                s = lax.dot_general(
                    kv_ref[0, k0:k1, :],
                    q_ref[q0 : q0 + tile, h * HEAD : (h + 1) * HEAD],
                    NT,
                    preferred_element_type=jnp.float32,
                )
                if first:
                    if q0 not in masks:
                        masks[q0] = allowed_pairs(q0, q0 + tile, k0, k1)
                    s = jnp.where(masks[q0], s, FAR_BELOW)
                elif masked:
                    if h == 0:
                        allowed = allowed_pairs(q0, q0 + tile, k0, k1)
                        bias_ref[k0:k1, q0 : q0 + tile] = jnp.where(allowed, 0.0, FAR_BELOW)
                    s = s + bias_ref[k0:k1, q0 : q0 + tile]
                scores[step] = s
            if 1 <= step <= len(items):
                h, q0, k0, k1 = items[step - 1]
                s = scores.pop(step - 1)
                top = jnp.max(s, axis=0, keepdims=True) if first else stat_in[h, 0:1, q0 : q0 + tile]
                tops[step - 1] = top
                if not masked:
                    top = jnp.where(low_ref[0:1, q0 : q0 + tile] <= first_key, top, -FAR_BELOW)
                weights[step - 1] = jnp.exp2((s - top) * EXP2_SCALE).astype(jnp.bfloat16)
            if 2 <= step:
                h, q0, k0, k1 = items[step - 2]
                q1 = q0 + tile
                sums = lax.dot_general(
                    vt_ref[:, k0:k1], weights.pop(step - 2), NN, preferred_element_type=jnp.float32
                )
                mixed = sums[:HEAD]
                total = sums[HEAD : HEAD + 1]
                if not first:
                    worst = jnp.maximum(worst, total)
                    mixed = mixed + acc_in[h * HEAD : (h + 1) * HEAD, q0:q1]
                    total = total + stat_in[h, 1:2, q0:q1]
                finish(h, q0, q1, mixed, total, tops.pop(step - 2))
        if not first:
            pl.when(jnp.logical_not(jnp.max(worst) < LIMIT))(rescaled)

    def rescaled():
        allowed = allowed_pairs(0, rows, 0, rows)

        def one_head(h, carry):
            hs = pl.ds(pl.multiple_of(h * HEAD, HEAD), HEAD)
            s = lax.dot_general(kv_ref[0], q_ref[:, hs], NT, preferred_element_type=jnp.float32)
            s = jnp.where(allowed, s, FAR_BELOW)
            old = stat_in[h, 0:1, :]
            top = jnp.maximum(old, jnp.max(s, axis=0, keepdims=True))
            factor = jnp.exp2((old - top) * EXP2_SCALE)
            p = jnp.exp2((s - top) * EXP2_SCALE).astype(jnp.bfloat16)
            sums = lax.dot_general(vt_ref[...], p, NN, preferred_element_type=jnp.float32)
            mixed = sums[:HEAD] + acc_in[hs, :] * factor
            total = sums[HEAD : HEAD + 1] + stat_in[h, 1:2, :] * factor
            finish(h, 0, rows, mixed, total, top)
            return carry

        lax.fori_loop(0, heads, one_head, 0)

    def keep():
        def one_head(h, carry):
            hs = pl.ds(pl.multiple_of(h * HEAD, HEAD), HEAD)
            finish(h, 0, rows, acc_in[hs, :], stat_in[h, 1:2, :], stat_in[h, 0:1, :])
            return carry

        lax.fori_loop(0, heads, one_head, 0)

    def work(masked):
        vt_ref[:HEAD, :] = kv_ref[1].T
        vt_ref[HEAD:, :] = jnp.ones((ONES, rows), vt_ref.dtype)
        flow(masked)

    if first:
        work(True)
        return
    low = low_ref[...]
    needed = jnp.min(low) < first_key + rows
    if window:
        whole = jnp.bool_(False)
    else:
        cut = (low > first_key) & (low < first_key + rows)
        whole = jnp.max(jnp.where(cut, 1.0, 0.0)) < 0.5
        pl.when(needed & whole)(functools.partial(work, False))
    pl.when(needed & jnp.logical_not(whole))(functools.partial(work, True))
    pl.when(jnp.logical_not(needed))(keep)


def take_in(backs, first, last, window, low, queries, kv, state, name):
    rows, width = queries.shape
    heads = width // HEAD
    state = () if first else state
    if last:
        out_shape = jax.ShapeDtypeStruct((rows, width), jnp.bfloat16)
        out_specs = VMEM
    else:
        out_shape = (
            jax.ShapeDtypeStruct((width, rows), jnp.float32),
            jax.ShapeDtypeStruct((heads, 8, rows), jnp.float32),
        )
        out_specs = (VMEM, VMEM)
    return pl.pallas_call(
        functools.partial(stage, backs, first, last, window, heads, rows),
        out_shape=out_shape,
        in_specs=[VMEM] * (3 + len(state)),
        out_specs=out_specs,
        scratch_shapes=[pltpu.VMEM((HEAD + ONES, rows), jnp.bfloat16), pltpu.VMEM((rows, rows), jnp.float32)],
        compiler_params=pltpu.CompilerParams(vmem_limit_bytes=32 * 1024 * 1024),
        cost_estimate=pl.CostEstimate(
            flops=4 * rows * rows * width,
            bytes_accessed=8 * rows * width,
            transcendentals=rows * rows * heads,
        ),
        name=name,
    )(low, queries, kv, *state)


def shards(queries, keys, values, doc_lengths):
    reach = lax.axis_size("inner")
    count = lax.axis_size(SEQ_AXES)
    rows = queries.shape[0]
    evens = range(2, reach - 1, 2)
    kv = jnp.stack([keys, values])
    low = query_lows(doc_lengths, rows)
    shift = {k: sent(kv, [(d, d + k) for d in range(count - k)]) for k in evens}
    kv, low = lax.optimization_barrier((kv, low))
    beside = sent(kv, [(d, d + (reach - 1 if d % 2 else 1)) for d in range(count) if d % 2 == 0 or d + reach - 1 < count])
    window = sent(kv, [(d, d + reach) for d in range(count - reach)])
    state = take_in((0, 0), True, False, False, low, queries, kv, None, "take_own")
    state = take_in((reach, reach), False, False, True, low, queries, window, state, "take_window")
    swap = {k: sent(shift[k], [(d, d + 1 - 2 * (d % 2)) for d in range(k, count)]) for k in evens}
    state = take_in((reach - 1, 1), False, False, False, low, queries, beside, state, "take_beside")
    for k in evens:
        state = take_in((k, k), False, False, False, low, queries, shift[k], state, "take_shift")
        state = take_in((k - 1, k + 1), False, k == evens[-1], False, low, queries, swap[k], state, "take_swap")
    return state


def solution(mesh):
    return jax.shard_map(
        shards,
        mesh=mesh,
        in_specs=(
            P(("groups", "outer", "inner"), None),
            P(("groups", "outer", "inner"), None),
            P(("groups", "outer", "inner"), None),
            P("groups"),
        ),
        out_specs=P(("groups", "outer", "inner"), None),
        check_vma=False,
    )
```

```python
import functools
import math

import jax
import jax.numpy as jnp
from jax import lax
from jax.experimental import pallas as pl
from jax.experimental.pallas import tpu as pltpu
from jax.sharding import PartitionSpec as P

HEAD = 128
ONES = 16
FAR_BELOW = -1e30
LIMIT = 2.0**60
EXP2_SCALE = math.log2(math.e) / math.sqrt(HEAD)
SEQ_AXES = ("outer", "inner")
VMEM = pl.BlockSpec(memory_space=pltpu.VMEM)
NT = (((1,), (1,)), ((), ()))
NN = (((1,), (0,)), ((), ()))


def sent(value, pairs):
    return lax.ppermute(value, SEQ_AXES, pairs)


def document_starts(docs_ref, low_out):
    first_row = lax.axis_index(SEQ_AXES) * low_out.shape[1]
    position = first_row + lax.broadcasted_iota(jnp.int32, low_out.shape, 1)
    end = jnp.int32(0)
    start = jnp.zeros_like(position)
    for doc in range(docs_ref.shape[0]):
        end = end + docs_ref[doc]
        start = jnp.where(position >= end, end, start)
    low_out[...] = (start - first_row).astype(jnp.float32)


def query_lows(docs, rows):
    return pl.pallas_call(
        document_starts,
        out_shape=jax.ShapeDtypeStruct((8, rows), jnp.float32),
        in_specs=[pl.BlockSpec(memory_space=pltpu.SMEM)],
        out_specs=VMEM,
        compiler_params=pltpu.CompilerParams(vmem_limit_bytes=8 * 1024 * 1024),
        name="document_starts",
    )(docs)


def stage(backs, first, last, window, heads, tile, *refs):
    low_ref, q_ref, kv_ref, *refs = refs
    if not first:
        acc_in, stat_in, *refs = refs
    if last:
        out_ref, vt_ref, bias_ref = refs
    else:
        acc_out, stat_out, vt_ref, bias_ref = refs
    rows = q_ref.shape[0]
    if backs[0] == backs[1]:
        back = backs[0]
    else:
        back = backs[0] + (backs[1] - backs[0]) * lax.rem(lax.axis_index("inner"), 2)
    first_key = (-back * rows) if isinstance(back, int) else (-back * rows).astype(jnp.float32)

    def allowed_pairs(q0, q1, k0, k1):
        low = low_ref[0:1, q0:q1].astype(jnp.int32) + (back * rows - k0)
        key = lax.broadcasted_iota(jnp.int32, (k1 - k0, q1 - q0), 0)
        allowed = key >= low
        if first:
            query = q0 - k0 + lax.broadcasted_iota(jnp.int32, (1, q1 - q0), 1)
            allowed = allowed & (key <= query)
        return allowed

    def finish(h, q0, q1, mixed, total, top):
        if isinstance(h, int):
            hs = slice(h * HEAD, (h + 1) * HEAD)
        else:
            hs = pl.ds(pl.multiple_of(h * HEAD, HEAD), HEAD)
        if last:
            out_ref[q0:q1, hs] = (mixed * (1.0 / total)).astype(out_ref.dtype).T
        else:
            acc_out[hs, q0:q1] = mixed
            stat_out[h, 0:1, q0:q1] = top
            stat_out[h, 1:2, q0:q1] = total

    def flow(masked):
        items = []
        for h in range(heads):
            for q0 in range(0, rows, tile):
                k0 = q0 if window else 0
                k1 = q0 + tile if first else rows
                items.append((h, q0, k0, k1))
        masks, scores, weights, tops = {}, {}, {}, {}
        worst = jnp.zeros((1, tile), jnp.float32)
        for step in range(len(items) + 2):
            if step < len(items):
                h, q0, k0, k1 = items[step]
                s = lax.dot_general(
                    kv_ref[0, k0:k1, :],
                    q_ref[q0 : q0 + tile, h * HEAD : (h + 1) * HEAD],
                    NT,
                    preferred_element_type=jnp.float32,
                )
                if first:
                    if q0 not in masks:
                        masks[q0] = allowed_pairs(q0, q0 + tile, k0, k1)
                    s = jnp.where(masks[q0], s, FAR_BELOW)
                elif masked:
                    if h == 0:
                        allowed = allowed_pairs(q0, q0 + tile, k0, k1)
                        bias_ref[k0:k1, q0 : q0 + tile] = jnp.where(allowed, 0.0, FAR_BELOW)
                    s = s + bias_ref[k0:k1, q0 : q0 + tile]
                scores[step] = s
            if 1 <= step <= len(items):
                h, q0, k0, k1 = items[step - 1]
                s = scores.pop(step - 1)
                top = jnp.max(s, axis=0, keepdims=True) if first else stat_in[h, 0:1, q0 : q0 + tile]
                tops[step - 1] = top
                if not masked:
                    top = jnp.where(low_ref[0:1, q0 : q0 + tile] <= first_key, top, -FAR_BELOW)
                weights[step - 1] = jnp.exp2((s - top) * EXP2_SCALE).astype(jnp.bfloat16)
            if 2 <= step:
                h, q0, k0, k1 = items[step - 2]
                q1 = q0 + tile
                sums = lax.dot_general(
                    vt_ref[:, k0:k1], weights.pop(step - 2), NN, preferred_element_type=jnp.float32
                )
                mixed = sums[:HEAD]
                total = sums[HEAD : HEAD + 1]
                if not first:
                    worst = jnp.maximum(worst, total)
                    mixed = mixed + acc_in[h * HEAD : (h + 1) * HEAD, q0:q1]
                    total = total + stat_in[h, 1:2, q0:q1]
                finish(h, q0, q1, mixed, total, tops.pop(step - 2))
        if not first:
            pl.when(jnp.logical_not(jnp.max(worst) < LIMIT))(rescaled)

    def rescaled():
        allowed = allowed_pairs(0, rows, 0, rows)

        def one_head(h, carry):
            hs = pl.ds(pl.multiple_of(h * HEAD, HEAD), HEAD)
            s = lax.dot_general(kv_ref[0], q_ref[:, hs], NT, preferred_element_type=jnp.float32)
            s = jnp.where(allowed, s, FAR_BELOW)
            old = stat_in[h, 0:1, :]
            top = jnp.maximum(old, jnp.max(s, axis=0, keepdims=True))
            factor = jnp.exp2((old - top) * EXP2_SCALE)
            p = jnp.exp2((s - top) * EXP2_SCALE).astype(jnp.bfloat16)
            sums = lax.dot_general(vt_ref[...], p, NN, preferred_element_type=jnp.float32)
            mixed = sums[:HEAD] + acc_in[hs, :] * factor
            total = sums[HEAD : HEAD + 1] + stat_in[h, 1:2, :] * factor
            finish(h, 0, rows, mixed, total, top)
            return carry

        lax.fori_loop(0, heads, one_head, 0)

    def keep():
        def one_head(h, carry):
            hs = pl.ds(pl.multiple_of(h * HEAD, HEAD), HEAD)
            finish(h, 0, rows, acc_in[hs, :], stat_in[h, 1:2, :], stat_in[h, 0:1, :])
            return carry

        lax.fori_loop(0, heads, one_head, 0)

    def work(masked):
        vt_ref[:HEAD, :] = kv_ref[1].T
        vt_ref[HEAD:, :] = jnp.ones((ONES, rows), vt_ref.dtype)
        flow(masked)

    if first:
        work(True)
        return
    low = low_ref[...]
    needed = jnp.min(low) < first_key + rows
    if window:
        whole = jnp.bool_(False)
    else:
        cut = (low > first_key) & (low < first_key + rows)
        whole = jnp.max(jnp.where(cut, 1.0, 0.0)) < 0.5
        pl.when(needed & whole)(functools.partial(work, False))
    pl.when(needed & jnp.logical_not(whole))(functools.partial(work, True))
    pl.when(jnp.logical_not(needed))(keep)


def take_in(backs, first, last, window, low, queries, kv, state, name):
    rows, width = queries.shape
    heads = width // HEAD
    state = () if first else state
    if last:
        out_shape = jax.ShapeDtypeStruct((rows, width), jnp.bfloat16)
        out_specs = VMEM
    else:
        out_shape = (
            jax.ShapeDtypeStruct((width, rows), jnp.float32),
            jax.ShapeDtypeStruct((heads, 8, rows), jnp.float32),
        )
        out_specs = (VMEM, VMEM)
    return pl.pallas_call(
        functools.partial(stage, backs, first, last, window, heads, rows),
        out_shape=out_shape,
        in_specs=[VMEM] * (3 + len(state)),
        out_specs=out_specs,
        scratch_shapes=[pltpu.VMEM((HEAD + ONES, rows), jnp.bfloat16), pltpu.VMEM((rows, rows), jnp.float32)],
        compiler_params=pltpu.CompilerParams(vmem_limit_bytes=32 * 1024 * 1024),
        cost_estimate=pl.CostEstimate(
            flops=4 * rows * rows * width,
            bytes_accessed=8 * rows * width,
            transcendentals=rows * rows * heads,
        ),
        name=name,
    )(low, queries, kv, *state)


def shards(queries, keys, values, doc_lengths):
    reach = lax.axis_size("inner")
    count = lax.axis_size(SEQ_AXES)
    rows = queries.shape[0]
    evens = range(2, reach - 1, 2)
    kv = jnp.stack([keys, values])
    low = query_lows(doc_lengths, rows)
    shift = {k: sent(kv, [(d, d + k) for d in range(count - k)]) for k in evens}
    kv, low = lax.optimization_barrier((kv, low))
    beside = sent(kv, [(d, d + (reach - 1 if d % 2 else 1)) for d in range(count) if d % 2 == 0 or d + reach - 1 < count])
    window = sent(kv, [(d, d + reach) for d in range(count - reach)])
    state = take_in((0, 0), True, False, False, low, queries, kv, None, "take_own")
    swap = {k: sent(shift[k], [(d, d + 1 - 2 * (d % 2)) for d in range(k, count)]) for k in evens}
    for k in evens:
        state = take_in((k, k), False, False, False, low, queries, shift[k], state, "take_shift")
    state = take_in((reach - 1, 1), False, False, False, low, queries, beside, state, "take_beside")
    state = take_in((reach, reach), False, False, True, low, queries, window, state, "take_window")
    for k in evens:
        state = take_in((k - 1, k + 1), False, k == evens[-1], False, low, queries, swap[k], state, "take_swap")
    return state


def solution(mesh):
    return jax.shard_map(
        shards,
        mesh=mesh,
        in_specs=(
            P(("groups", "outer", "inner"), None),
            P(("groups", "outer", "inner"), None),
            P(("groups", "outer", "inner"), None),
            P("groups"),
        ),
        out_specs=P(("groups", "outer", "inner"), None),
        check_vma=False,
    )
```

```python
import functools
import math

import jax
import jax.numpy as jnp
from jax import lax
from jax.experimental import pallas as pl
from jax.experimental.pallas import tpu as pltpu
from jax.sharding import PartitionSpec as P

HEAD = 128
ONES = 16
FAR_BELOW = -1e30
LIMIT = 2.0**60
EXP2_SCALE = math.log2(math.e) / math.sqrt(HEAD)
SEQ_AXES = ("outer", "inner")
VMEM = pl.BlockSpec(memory_space=pltpu.VMEM)
NT = (((1,), (1,)), ((), ()))
NN = (((1,), (0,)), ((), ()))


def sent(value, pairs):
    return lax.ppermute(value, SEQ_AXES, pairs)


def document_starts(docs_ref, low_out):
    first_row = lax.axis_index(SEQ_AXES) * low_out.shape[1]
    position = first_row + lax.broadcasted_iota(jnp.int32, low_out.shape, 1)
    end = jnp.int32(0)
    start = jnp.zeros_like(position)
    for doc in range(docs_ref.shape[0]):
        end = end + docs_ref[doc]
        start = jnp.where(position >= end, end, start)
    low_out[...] = (start - first_row).astype(jnp.float32)


def query_lows(docs, rows):
    return pl.pallas_call(
        document_starts,
        out_shape=jax.ShapeDtypeStruct((8, rows), jnp.float32),
        in_specs=[pl.BlockSpec(memory_space=pltpu.SMEM)],
        out_specs=VMEM,
        compiler_params=pltpu.CompilerParams(vmem_limit_bytes=8 * 1024 * 1024),
        name="document_starts",
    )(docs)


def stage(backs, first, last, window, heads, tile, *refs):
    low_ref, q_ref, kv_ref, *refs = refs
    if not first:
        acc_in, stat_in, *refs = refs
    if last:
        out_hbm, vt_ref, bias_ref, out_ref, sems = refs
    else:
        acc_out, stat_out, vt_ref, bias_ref = refs
    rows = q_ref.shape[0]
    if backs[0] == backs[1]:
        back = backs[0]
    else:
        back = backs[0] + (backs[1] - backs[0]) * lax.rem(lax.axis_index("inner"), 2)
    first_key = (-back * rows) if isinstance(back, int) else (-back * rows).astype(jnp.float32)

    def allowed_pairs(q0, q1, k0, k1):
        low = low_ref[0:1, q0:q1].astype(jnp.int32) + (back * rows - k0)
        key = lax.broadcasted_iota(jnp.int32, (k1 - k0, q1 - q0), 0)
        allowed = key >= low
        if first:
            query = q0 - k0 + lax.broadcasted_iota(jnp.int32, (1, q1 - q0), 1)
            allowed = allowed & (key <= query)
        return allowed

    def written(h, hs):
        return pltpu.make_async_copy(out_ref.at[:, hs], out_hbm.at[:, hs], sems.at[h])

    def wait_written():
        if last:
            for h in range(heads):
                written(h, slice(h * HEAD, (h + 1) * HEAD)).wait()

    def finish(h, q0, q1, mixed, total, top):
        if isinstance(h, int):
            hs = slice(h * HEAD, (h + 1) * HEAD)
        else:
            hs = pl.ds(pl.multiple_of(h * HEAD, HEAD), HEAD)
        if last:
            out_ref[q0:q1, hs] = (mixed * (1.0 / total)).astype(out_ref.dtype).T
            written(h, hs).start()
        else:
            acc_out[hs, q0:q1] = mixed
            stat_out[h, 0:1, q0:q1] = top
            stat_out[h, 1:2, q0:q1] = total

    def flow(masked):
        items = []
        for h in range(heads):
            for q0 in range(0, rows, tile):
                k0 = q0 if window else 0
                k1 = q0 + tile if first else rows
                items.append((h, q0, k0, k1))
        masks, scores, weights, tops = {}, {}, {}, {}
        worst = jnp.zeros((1, tile), jnp.float32)
        for step in range(len(items) + 2):
            if step < len(items):
                h, q0, k0, k1 = items[step]
                s = lax.dot_general(
                    kv_ref[0, k0:k1, :],
                    q_ref[q0 : q0 + tile, h * HEAD : (h + 1) * HEAD],
                    NT,
                    preferred_element_type=jnp.float32,
                )
                if first:
                    if q0 not in masks:
                        masks[q0] = allowed_pairs(q0, q0 + tile, k0, k1)
                    s = jnp.where(masks[q0], s, FAR_BELOW)
                elif masked:
                    if h == 0:
                        allowed = allowed_pairs(q0, q0 + tile, k0, k1)
                        bias_ref[k0:k1, q0 : q0 + tile] = jnp.where(allowed, 0.0, FAR_BELOW)
                    s = s + bias_ref[k0:k1, q0 : q0 + tile]
                scores[step] = s
            if 1 <= step <= len(items):
                h, q0, k0, k1 = items[step - 1]
                s = scores.pop(step - 1)
                top = jnp.max(s, axis=0, keepdims=True) if first else stat_in[h, 0:1, q0 : q0 + tile]
                tops[step - 1] = top
                if not masked:
                    top = jnp.where(low_ref[0:1, q0 : q0 + tile] <= first_key, top, -FAR_BELOW)
                weights[step - 1] = jnp.exp2((s - top) * EXP2_SCALE).astype(jnp.bfloat16)
            if 2 <= step:
                h, q0, k0, k1 = items[step - 2]
                q1 = q0 + tile
                sums = lax.dot_general(
                    vt_ref[:, k0:k1], weights.pop(step - 2), NN, preferred_element_type=jnp.float32
                )
                mixed = sums[:HEAD]
                total = sums[HEAD : HEAD + 1]
                if not first:
                    worst = jnp.maximum(worst, total)
                    mixed = mixed + acc_in[h * HEAD : (h + 1) * HEAD, q0:q1]
                    total = total + stat_in[h, 1:2, q0:q1]
                finish(h, q0, q1, mixed, total, tops.pop(step - 2))
        if not first:
            rescale = jnp.logical_not(jnp.max(worst) < LIMIT)
            wait_written()
            pl.when(rescale)(rescaled)

    def rescaled():
        allowed = allowed_pairs(0, rows, 0, rows)

        def one_head(h, carry):
            hs = pl.ds(pl.multiple_of(h * HEAD, HEAD), HEAD)
            s = lax.dot_general(kv_ref[0], q_ref[:, hs], NT, preferred_element_type=jnp.float32)
            s = jnp.where(allowed, s, FAR_BELOW)
            old = stat_in[h, 0:1, :]
            top = jnp.maximum(old, jnp.max(s, axis=0, keepdims=True))
            factor = jnp.exp2((old - top) * EXP2_SCALE)
            p = jnp.exp2((s - top) * EXP2_SCALE).astype(jnp.bfloat16)
            sums = lax.dot_general(vt_ref[...], p, NN, preferred_element_type=jnp.float32)
            mixed = sums[:HEAD] + acc_in[hs, :] * factor
            total = sums[HEAD : HEAD + 1] + stat_in[h, 1:2, :] * factor
            finish(h, 0, rows, mixed, total, top)
            return carry

        lax.fori_loop(0, heads, one_head, 0)
        wait_written()

    def keep():
        def one_head(h, carry):
            hs = pl.ds(pl.multiple_of(h * HEAD, HEAD), HEAD)
            finish(h, 0, rows, acc_in[hs, :], stat_in[h, 1:2, :], stat_in[h, 0:1, :])
            return carry

        lax.fori_loop(0, heads, one_head, 0)
        wait_written()

    def work(masked):
        vt_ref[:HEAD, :] = kv_ref[1].T
        vt_ref[HEAD:, :] = jnp.ones((ONES, rows), vt_ref.dtype)
        flow(masked)

    if first:
        work(True)
        return
    low = low_ref[...]
    needed = jnp.min(low) < first_key + rows
    if window:
        whole = jnp.bool_(False)
    else:
        cut = (low > first_key) & (low < first_key + rows)
        whole = jnp.max(jnp.where(cut, 1.0, 0.0)) < 0.5
        pl.when(needed & whole)(functools.partial(work, False))
    pl.when(needed & jnp.logical_not(whole))(functools.partial(work, True))
    pl.when(jnp.logical_not(needed))(keep)


def take_in(backs, first, last, window, low, queries, kv, state, name):
    rows, width = queries.shape
    heads = width // HEAD
    state = () if first else state
    if last:
        out_shape = jax.ShapeDtypeStruct((rows, width), jnp.bfloat16)
        out_specs = pl.BlockSpec(memory_space=pl.ANY)
        scratch = [pltpu.VMEM((rows, width), jnp.bfloat16), pltpu.SemaphoreType.DMA((heads,))]
    else:
        scratch = []
        out_shape = (
            jax.ShapeDtypeStruct((width, rows), jnp.float32),
            jax.ShapeDtypeStruct((heads, 8, rows), jnp.float32),
        )
        out_specs = (VMEM, VMEM)
    return pl.pallas_call(
        functools.partial(stage, backs, first, last, window, heads, rows),
        out_shape=out_shape,
        in_specs=[VMEM] * (3 + len(state)),
        out_specs=out_specs,
        scratch_shapes=[pltpu.VMEM((HEAD + ONES, rows), jnp.bfloat16), pltpu.VMEM((rows, rows), jnp.float32)] + scratch,
        compiler_params=pltpu.CompilerParams(vmem_limit_bytes=32 * 1024 * 1024),
        cost_estimate=pl.CostEstimate(
            flops=4 * rows * rows * width,
            bytes_accessed=8 * rows * width,
            transcendentals=rows * rows * heads,
        ),
        name=name,
    )(low, queries, kv, *state)


def shards(queries, keys, values, doc_lengths):
    reach = lax.axis_size("inner")
    count = lax.axis_size(SEQ_AXES)
    rows = queries.shape[0]
    evens = range(2, reach - 1, 2)
    kv = jnp.stack([keys, values])
    low = query_lows(doc_lengths, rows)
    shift = {k: sent(kv, [(d, d + k) for d in range(count - k)]) for k in evens}
    beside = sent(kv, [(d, d + (reach - 1 if d % 2 else 1)) for d in range(count) if d % 2 == 0 or d + reach - 1 < count])
    state = take_in((0, 0), True, False, False, low, queries, kv, None, "take_own")
    swap = {k: sent(shift[k], [(d, d + 1 - 2 * (d % 2)) for d in range(k, count)]) for k in evens}
    kv, state = lax.optimization_barrier((kv, state))
    window = sent(kv, [(d, d + reach) for d in range(count - reach)])
    for k in evens:
        state = take_in((k, k), False, False, False, low, queries, shift[k], state, "take_shift")
    state = take_in((reach - 1, 1), False, False, False, low, queries, beside, state, "take_beside")
    state = take_in((reach, reach), False, False, True, low, queries, window, state, "take_window")
    for k in evens:
        state = take_in((k - 1, k + 1), False, k == evens[-1], False, low, queries, swap[k], state, "take_swap")
    return state


def solution(mesh):
    return jax.shard_map(
        shards,
        mesh=mesh,
        in_specs=(
            P(("groups", "outer", "inner"), None),
            P(("groups", "outer", "inner"), None),
            P(("groups", "outer", "inner"), None),
            P("groups"),
        ),
        out_specs=P(("groups", "outer", "inner"), None),
        check_vma=False,
    )
```
